128 devices in a mesh: dp: 4 (over y), tensor: 32 (over x, z, core).
Axes of the slice: x: 4, y: 4, z: 4, core: 2. Of those that a mesh axis runs over, the one named last changes fastest.
Arguments:
- hidden_input: bfloat16 [4096, 29568], P('dp', 'tensor'), may hold values from -6 to 6
- output_gradient: bfloat16 [4096, 8192], P('dp', 'tensor'), may hold values from -6 to 6
- frozen_weight: bfloat16 [29568, 8192], P('tensor'), may hold values from -0.03125 to 0.03125
- adapter_down: float32 [29568, 128], P('tensor'), may hold values from -0.773465 to 0.773465, as said below
- adapter_up: float32 [128, 8192], P(None, 'tensor'), may hold values from -1.4694563 to 1.4694563, as said below
Outputs:
- input_grad: bfloat16 [4096, 29568], P('dp', 'tensor')
- step_down: float32 [29568, 128], P('tensor')
- step_up: float32 [128, 8192], P(None, 'tensor')
The draws below stay inside these ranges and needn't reach their ends.
Inputs may be any that keep to these rules, and one draw needn't show every extreme that they name: `adapter_down`: a trained adapter factor. `adapter_up`: a trained adapter factor.
All inputs are finite; a program needn't handle non-finite values.
Results may differ from the reference program's by a relative error of at most 0.0064.
Values may be sent and summed in bfloat16 or wider, within the bound.
A program may use at most 128 MiB of HBM per device.

```python
import jax
import jax.numpy as jnp
from jax import lax

D = 8192
FF = 29568
R = 128
TOKENS = 4096


def scaled_factor(key, rows, cols, rise_rows, fan):
    k_base, k_row, k_col = jax.random.split(key, 3)
    row_scale = jnp.exp(jax.random.uniform(k_row, (rows, 1), jnp.float32, -1.2, 1.2))
    col_scale = jnp.exp(jax.random.uniform(k_col, (1, cols), jnp.float32, -1.2, 1.2))
    if rise_rows:
        row_scale = row_scale * (3.0 ** (jnp.arange(rows, dtype=jnp.float32) / rows))[:, None]
    else:
        col_scale = col_scale * (3.0 ** (jnp.arange(cols, dtype=jnp.float32) / cols))[None, :]
    base = jnp.clip(jax.random.normal(k_base, (rows, cols), jnp.float32), -4.0, 4.0)
    return base * row_scale * col_scale / jnp.sqrt(jnp.float32(fan))


def draw_adapter_down(key, part):
    key = jax.random.fold_in(key, 11)
    return scaled_factor(key, FF, R, True, FF)


def draw_adapter_up(key, part):
    key = jax.random.fold_in(key, 23)
    return scaled_factor(key, R, D, False, D)


def steps_of(own_key, dims, shards, smallest, top_value):
    factor_of, own = 1.0, jax.random.fold_in(own_key, 6)
    for dim, blocks in shards:
        heights = jnp.exp(jax.random.uniform(jax.random.fold_in(own, dim), (blocks,), jnp.float32, smallest / len(shards), top_value / len(shards)))
        factor_of = factor_of * jnp.repeat(heights, dims[dim] // blocks).reshape([-1 if axis == dim else 1 for axis in range(len(dims))])
    return factor_of


def bell_draw(rng, shape, spread, limit, pieces=(), kind=jnp.bfloat16):
    array = spread * jax.random.normal(rng, shape, jnp.float32)
    if pieces:
        array = array * steps_of(rng, shape, pieces, -0.22, 0.18)
    return jnp.clip(array, -limit, limit).astype(kind)


def setup_inputs(seed: int = 0) -> dict:
    splits = jax.random.split(jax.random.key(seed), 6)
    return {
        "hidden_input": bell_draw(splits[0], (TOKENS, FF), 1.0, 6.0, ((0, 4), (1, 32))),
        "output_gradient": bell_draw(splits[1], (TOKENS, D), 1.0, 6.0, ((0, 4), (1, 32))),
        "frozen_weight": bell_draw(splits[2], (FF, D), FF ** -0.5, 0.03125, ((0, 32),)),
        "adapter_down": draw_adapter_down(jax.random.fold_in(splits[5], 71), 0),
        "adapter_up": draw_adapter_up(jax.random.fold_in(splits[5], 71), 0),
    }


SCALE = 2.0
RATE = 0.01
DAMPING = 0.01

def contract(left, right, dims_left, dims_right):
    return lax.dot_general(left.astype(jnp.float32), right.astype(jnp.float32), (((dims_left,), (dims_right,)), ((), ())), preferred_element_type=jnp.float32)

def reference(hidden_input, output_gradient, frozen_weight, adapter_down, adapter_up):
    down_factor_half = adapter_down.astype(jnp.bfloat16)
    up_factor_half = adapter_up.astype(jnp.bfloat16)
    rank_input = jnp.dot(hidden_input.astype(jnp.float32), down_factor_half.astype(jnp.float32), preferred_element_type=jnp.float32)
    rank_cotangent = contract(output_gradient, up_factor_half, 1, 1)
    input16 = rank_input.astype(jnp.bfloat16)
    cotangent16 = rank_cotangent.astype(jnp.bfloat16)
    base_term = contract(output_gradient, frozen_weight, 1, 1)
    input_grad = (base_term + SCALE * contract(cotangent16, down_factor_half, 1, 1)).astype(jnp.bfloat16)
    grad_down = SCALE * contract(hidden_input, cotangent16, 0, 0)
    grad_up = SCALE * contract(input16, output_gradient, 0, 0)
    down_gram_matrix = jnp.dot(adapter_down.T, adapter_down, precision=lax.Precision.HIGHEST)
    up_gram_matrix = jnp.dot(adapter_up, adapter_up.T, precision=lax.Precision.HIGHEST)
    identity = jnp.eye(up_gram_matrix.shape[0], dtype=jnp.float32)
    chol_up = jnp.linalg.cholesky(up_gram_matrix + DAMPING * identity)
    chol_down = jnp.linalg.cholesky(down_gram_matrix + DAMPING * identity)
    step_down = RATE * jax.scipy.linalg.cho_solve((chol_up, True), grad_down.T).T
    step_up = RATE * jax.scipy.linalg.cho_solve((chol_down, True), grad_up)
    return (input_grad, step_down, step_up)
```

```python
import jax
import jax.numpy as jnp
from jax import lax
from jax.experimental import pallas as pl
from jax.experimental.pallas import tpu as pltpu
from jax.sharding import PartitionSpec as P

SCALE = 2.0
RATE = 0.01
DAMPING = 0.01
RANK = 128
TOKENS = 1024
COLS = 256
HIDDEN = 924
SLOTS = 32
CHUNKS = 2
CHUNK = TOKENS // CHUNKS
DOWN_ROWS, UP_ROWS = 232, 64
STEP_ROWS = DOWN_ROWS + UP_ROWS
BLOCK = 72
MESH = pl.DeviceIdType.MESH
HIGHEST = lax.Precision.HIGHEST

ORDER = (
    (0, 0), (-1, 0), (1, 0), (0, -1), (0, 1), (2, 0), (0, 2), (-1, -1), (-1, 1),
    (-1, 2), (1, -1), (1, 1), (1, 2), (2, -1), (2, 1), (2, 2),
)
OWN_AT = {1: 0, 2: 0, 3: 2, 4: 2, 5: 3, 6: 4, 7: 5, 8: 6, 9: 7, 10: 8, 11: 9, 12: 10, 13: 12, 14: 13, 15: 14}
INVERT_FROM, INVERT_PER = 5, 2
STEPS = 16


def dot(left, right, dims_left, dims_right, precision=None):
    return lax.dot_general(
        left,
        right,
        (((dims_left,), (dims_right,)), ((), ())),
        precision=precision,
        preferred_element_type=jnp.float32,
    )


def eliminate(mat, count):
    lane = lax.broadcasted_iota(jnp.int32, (RANK, RANK), 1)
    row_of = lax.broadcasted_iota(jnp.int32, (RANK, RANK), 0)
    lane_row = lax.broadcasted_iota(jnp.int32, (1, RANK), 1)
    for j in range(count):
        column = jnp.broadcast_to(mat[:, j : j + 1], (RANK, RANK))
        inverse = 1.0 / column[j : j + 1, :]
        row = jnp.where(lane_row == j, inverse, mat[j : j + 1, :] * inverse)
        base = jnp.where((lane == j) | (row_of == j), 0.0, mat)
        mat = base - jnp.where(row_of == j, -1.0, column) * row
    mat = jnp.concatenate([mat[count:], mat[:count]], axis=0)
    return pltpu.roll(mat, RANK - count, axis=1)


def kernel(
    hidden_hbm, grad_hbm, weight_hbm, down_hbm, up_hbm,
    out_hbm, step_down_hbm, step_up_hbm,
    buf, weight, hidden, down, up, down16, acc, out16,
    part, from_sib, chip_sum, ring1, quarter, ring2, half16, gram,
    inverse, grads, grads_in, steps, step_up,
    local_sem, send_sem, slot_sem, misc_sem,
):
    dp = lax.axis_index("dp")
    me = lax.axis_index("tensor")
    core = lax.rem(me, 2)
    z = lax.rem(me // 2, 4)
    x = me // 8
    other = 1 - core
    a = x + core * (z - x)
    b = z + core * (x - z)

    def mod4(v):
        return lax.rem(v + 8, 4)

    def place(core_, a_, b_):
        return mod4(a_) * (8 - 6 * core_) + mod4(b_) * (2 + 6 * core_) + core_

    sib = me + 1 - 2 * core
    own = [place(core, a + da, b + db) for da, db in ORDER]
    theirs = [place(other, b + da, a + db) for da, db in ORDER]
    along_a = [(dp, place(core, a + d, b)) for d in (1, -1, 2)]
    along_b = [(dp, place(core, a, b + d)) for d in (1, -1, 2)]
    along_y = [(mod4(dp + d), me) for d in (1, -1, 2)]
    sibling = (dp, sib)
    a_plus, a_minus = along_a[0], along_a[1]
    b_plus, b_minus = along_b[0], along_b[1]

    def local(src, dst, sem):
        return pltpu.make_async_copy(src, dst, local_sem.at[sem])

    loads = [
        local(grad_hbm, buf.at[me], 0),
        local(up_hbm, up, 1),
        local(hidden_hbm, hidden, 2),
        local(down_hbm, down, 3),
        local(weight_hbm, weight, 4),
    ]
    for load in loads:
        load.start()

    barrier = pltpu.get_barrier_semaphore()
    partners = along_a + along_b + along_y + [sibling]
    for partner in partners:
        pl.semaphore_signal(barrier, inc=1, device_id=partner, device_id_type=MESH)
    pl.semaphore_wait(barrier, len(partners))

    pending = []

    def remote(refs, device):
        index = len(pending)

        def make(device):
            src, dst, recv_sem = refs()
            return pltpu.make_async_remote_copy(
                src_ref=src,
                dst_ref=dst,
                send_sem=send_sem.at[index],
                recv_sem=recv_sem,
                device_id=device,
                device_id_type=MESH,
            )

        pending.append(make)
        make(device).start()

    def landed(dst, recv_sem):
        pltpu.make_async_remote_copy(
            src_ref=dst,
            dst_ref=dst,
            send_sem=send_sem.at[0],
            recv_sem=recv_sem,
            device_id=sibling,
            device_id_type=MESH,
        ).wait_recv()

    def piece(slot, c):
        return buf.at[slot, pl.ds(c * CHUNK, CHUNK)]

    def pass_on(slot, c, device):
        remote(lambda: (piece(slot, c), piece(slot, c), slot_sem.at[slot, c]), device)

    def arrived(slot, c):
        landed(piece(slot, c), slot_sem.at[slot, c])

    SIB_PART, RING1, RING2, AG1_HALF, AG1_GRAM, AG2_HALF, AG2_GRAM = 0, 1, 4, 7, 10, 13, 16
    SIB_HALF, SIB_INV, Y_GRAD, Y_STEP = 19, 20, 21, 24

    loads[0].wait()
    for c in range(CHUNKS):
        pass_on(me, c, a_plus)
        pass_on(me, c, a_minus)

    loads[1].wait()
    up_f32 = up[...]
    part[0, :, 0:64, :] = dot(buf[me], up_f32.astype(jnp.bfloat16), 1, 1).reshape(16, 64, RANK)
    part[0, :, 64:BLOCK, :] = dot(up_f32, up_f32, 1, 1, HIGHEST).reshape(16, 8, RANK)
    loads[2].wait()
    loads[3].wait()
    down_f32 = down[...]
    down16[...] = down_f32.astype(jnp.bfloat16)
    part[1, :, 0:64, :] = dot(hidden[...], down16[...], 1, 0).reshape(16, 64, RANK)
    part[1, :, 64:BLOCK, :] = dot(down_f32, down_f32, 0, 0, HIGHEST).reshape(16, 8, RANK)
    remote(lambda: (part.at[other], from_sib, misc_sem.at[SIB_PART]), sibling)
    for c in range(CHUNKS):
        pass_on(me, c, sibling)
    acc[...] = jnp.zeros_like(acc)
    landed(from_sib, misc_sem.at[SIB_PART])
    for j, (d, device) in enumerate(zip((1, -1, 2, 0), along_a + [None])):
        rows = pl.ds(mod4(a + d) * 4, 4)
        chip_sum[rows] = part[core, rows] + from_sib[rows]
        if device is not None:
            remote(lambda j=j, rows=rows: (chip_sum.at[rows], ring1.at[j], misc_sem.at[RING1 + j]), device)
    pass_on(me, 0, b_plus)
    pass_on(me, 0, b_minus)
    loads[4].wait()

    def reduce_a():
        for j in range(3):
            landed(ring1.at[j], misc_sem.at[RING1 + j])
        quarter[...] = (chip_sum[pl.ds(a * 4, 4)] + ring1[0]) + (ring1[1] + ring1[2])
        for j, (d, device) in enumerate(zip((1, -1, 2), along_b)):
            remote(lambda j=j, d=d: (quarter.at[mod4(b + d)], ring2.at[j], misc_sem.at[RING2 + j]), device)
        pass_on(me, 1, b_plus)
        pass_on(me, 1, b_minus)

    mine = a * 4 + b

    def own_rows():
        return pl.ds(a * 4, 4)

    def reduce_b():
        for j in range(3):
            landed(ring2.at[j], misc_sem.at[RING2 + j])
        total = (quarter[b] + ring2[0]) + (ring2[1] + ring2[2])
        half16[core, mine] = total[0:64].astype(jnp.bfloat16)
        gram[mine] = total[64:BLOCK]
        for j, device in enumerate(along_b):
            remote(lambda j=j: (half16.at[core, mine], half16.at[core, mine], misc_sem.at[AG1_HALF + j]), device)
            remote(lambda j=j: (gram.at[mine], gram.at[mine], misc_sem.at[AG1_GRAM + j]), device)

    def gather_a():
        for j, d in enumerate((1, -1, 2)):
            block = a * 4 + mod4(b - d)
            landed(half16.at[core, block], misc_sem.at[AG1_HALF + j])
            landed(gram.at[block], misc_sem.at[AG1_GRAM + j])
        for j, device in enumerate(along_a):
            remote(lambda j=j: (half16.at[core, own_rows()], half16.at[core, own_rows()], misc_sem.at[AG2_HALF + j]), device)
            remote(lambda j=j: (gram.at[own_rows()], gram.at[own_rows()], misc_sem.at[AG2_GRAM + j]), device)

    def share_sib():
        for j, d in enumerate((1, -1, 2)):
            rows = pl.ds(mod4(a - d) * 4, 4)
            landed(half16.at[core, rows], misc_sem.at[AG2_HALF + j])
            landed(gram.at[rows], misc_sem.at[AG2_GRAM + j])
        remote(lambda: (half16.at[core], half16.at[core], misc_sem.at[SIB_HALF]), sibling)
        eye = lax.broadcasted_iota(jnp.int32, (RANK, RANK), 0) == lax.broadcasted_iota(
            jnp.int32, (RANK, RANK), 1
        )
        inverse[core] = gram[...].reshape(RANK, RANK) + jnp.where(eye, DAMPING, 0.0)

    def form_grads():
        landed(half16.at[other], misc_sem.at[SIB_HALF])
        cotangent16 = half16[0].reshape(TOKENS, RANK)
        input16 = half16[1].reshape(TOKENS, RANK)
        grad_down = SCALE * dot(cotangent16, hidden[...], 0, 0).T
        grad_up = SCALE * dot(input16, buf[me], 0, 0).T
        for q in range(4):
            last = min(DOWN_ROWS, HIDDEN - q * DOWN_ROWS)
            grads[q, 0:last] = grad_down[q * DOWN_ROWS : q * DOWN_ROWS + last]
            if last < DOWN_ROWS:
                grads[q, last:DOWN_ROWS] = jnp.zeros((DOWN_ROWS - last, RANK), jnp.float32)
            grads[q, DOWN_ROWS:STEP_ROWS] = grad_up[q * UP_ROWS : (q + 1) * UP_ROWS]
        for j, (d, device) in enumerate(zip((1, -1, 2), along_y)):
            remote(lambda j=j, d=d: (grads.at[mod4(dp + d)], grads_in.at[j], misc_sem.at[Y_GRAD + j]), device)
        acc[...] += dot(cotangent16 * jnp.bfloat16(SCALE), down16[...], 1, 1)

    def share_inverse():
        remote(lambda: (inverse.at[core], inverse.at[core], misc_sem.at[SIB_INV]), sibling)

    def solve():
        for j in range(3):
            landed(grads_in.at[j], misc_sem.at[Y_GRAD + j])
        total = RATE * ((grads[dp] + grads_in[0]) + (grads_in[1] + grads_in[2]))
        landed(inverse.at[other], misc_sem.at[SIB_INV])
        steps[dp, 0:DOWN_ROWS] = dot(total[0:DOWN_ROWS], inverse[0], 1, 0, HIGHEST)
        steps[dp, DOWN_ROWS:STEP_ROWS] = dot(total[DOWN_ROWS:STEP_ROWS], inverse[1], 1, 0, HIGHEST)
        for j, device in enumerate(along_y):
            remote(lambda j=j: (steps.at[dp], steps.at[dp], misc_sem.at[Y_STEP + j]), device)

    def spread(k):
        for c in range(CHUNKS):
            pass_on(own[k], c, b_plus)
            pass_on(own[k], c, b_minus)

    def receive(k):
        da, db = ORDER[k]
        for c in range(CHUNKS):
            arrived(own[k], c)
            if db == 0 and da == -1 and c == 0:
                pass_on(own[k], c, a_plus)
            if db == 0 and da == 1 and c == 1:
                pass_on(own[k], c, a_minus)
            if db == -1 and c == 0:
                pass_on(own[k], c, b_plus)
            if db == 1 and c == 1:
                pass_on(own[k], c, b_minus)
        if ORDER[k] == (2, 0):
            spread(k)
        for c in range(CHUNKS):
            pass_on(own[k], c, sibling)

    events = {i: [] for i in range(STEPS)}
    events[1].append(reduce_a)
    events[2].append(reduce_b)
    events[2].append(lambda: (spread(1), spread(2)))
    events[3].append(gather_a)
    for k in range(1, 16):
        events[OWN_AT[k]].append(lambda k=k: receive(k))
    events[4].append(share_sib)
    events[5].append(form_grads)
    events[13].append(share_inverse)
    events[14].append(solve)

    def pick(values, i):
        index = values[0]
        for k in range(1, len(values)):
            index = jnp.where(i == k, values[k], index)
        return index

    def step(i, carry):
        for k in range(STEPS):
            if events[k]:

                @pl.when(i == k)
                def _(k=k):
                    for event in events[k]:
                        event()

        slot_own, slot_sib = pick(own, i), pick(theirs, i)
        for c in range(CHUNKS):
            arrived(slot_sib, c)
        cols_own = pl.ds(pl.multiple_of(slot_own * COLS, COLS), COLS)
        cols_sib = pl.ds(pl.multiple_of(slot_sib * COLS, COLS), COLS)
        acc[...] += dot(buf[slot_own], weight[:, cols_own], 1, 1) + dot(
            buf[slot_sib], weight[:, cols_sib], 1, 1
        )

        @pl.when((i >= INVERT_FROM) & (i < INVERT_FROM + 16 // INVERT_PER))
        def _():
            mat = inverse[core]
            for _ in range(INVERT_PER):
                mat = eliminate(mat, 8)
            inverse[core] = mat

        return carry

    lax.fori_loop(0, STEPS, step, 0)

    out16[...] = acc[...].astype(jnp.bfloat16)
    stores = [local(out16, out_hbm, 0)]
    stores[0].start()
    for j, d in enumerate((1, -1, 2)):
        landed(steps.at[mod4(dp - d)], misc_sem.at[Y_STEP + j])
    for q in range(4):
        last = min(DOWN_ROWS, HIDDEN - q * DOWN_ROWS)
        store = local(
            steps.at[q, pl.ds(0, last)], step_down_hbm.at[pl.ds(q * DOWN_ROWS, last)], 1 + q
        )
        store.start()
        stores.append(store)
    step_up[...] = steps[:, DOWN_ROWS:STEP_ROWS, :].reshape(COLS, RANK).T
    stores.append(local(step_up, step_up_hbm, 5))
    stores[-1].start()
    for make in pending:
        make(sibling).wait_send()
    for store in stores:
        store.wait()


def per_device(hidden_input, output_gradient, frozen_weight, adapter_down, adapter_up):
    f32, bf16 = jnp.float32, jnp.bfloat16
    any_space = pl.BlockSpec(memory_space=pl.ANY)
    return pl.pallas_call(
        kernel,
        out_shape=(
            jax.ShapeDtypeStruct((TOKENS, HIDDEN), bf16),
            jax.ShapeDtypeStruct((HIDDEN, RANK), f32),
            jax.ShapeDtypeStruct((RANK, COLS), f32),
        ),
        in_specs=[any_space] * 5,
        out_specs=(any_space,) * 3,
        scratch_shapes=[
            pltpu.VMEM((SLOTS, TOKENS, COLS), bf16),
            pltpu.VMEM((HIDDEN, SLOTS * COLS), bf16),
            pltpu.VMEM((TOKENS, HIDDEN), bf16),
            pltpu.VMEM((HIDDEN, RANK), f32),
            pltpu.VMEM((RANK, COLS), f32),
            pltpu.VMEM((HIDDEN, RANK), bf16),
            pltpu.VMEM((TOKENS, HIDDEN), f32),
            pltpu.VMEM((TOKENS, HIDDEN), bf16),
            pltpu.VMEM((2, 16, BLOCK, RANK), f32),
            pltpu.VMEM((16, BLOCK, RANK), f32),
            pltpu.VMEM((16, BLOCK, RANK), f32),
            pltpu.VMEM((3, 4, BLOCK, RANK), f32),
            pltpu.VMEM((4, BLOCK, RANK), f32),
            pltpu.VMEM((3, BLOCK, RANK), f32),
            pltpu.VMEM((2, 16, 64, RANK), bf16),
            pltpu.VMEM((16, 8, RANK), f32),
            pltpu.VMEM((2, RANK, RANK), f32),
            pltpu.VMEM((4, STEP_ROWS, RANK), f32),
            pltpu.VMEM((3, STEP_ROWS, RANK), f32),
            pltpu.VMEM((4, STEP_ROWS, RANK), f32),
            pltpu.VMEM((RANK, COLS), f32),
            pltpu.SemaphoreType.DMA((6,)),
            pltpu.SemaphoreType.DMA((128,)),
            pltpu.SemaphoreType.DMA((SLOTS, CHUNKS)),
            pltpu.SemaphoreType.DMA((27,)),
        ],
        compiler_params=pltpu.CompilerParams(
            collective_id=0, has_side_effects=True, vmem_limit_bytes=60 * 2**20
        ),
    )(hidden_input, output_gradient, frozen_weight, adapter_down, adapter_up)


def solution(mesh):
    in_specs = (
        P("dp", "tensor"),
        P("dp", "tensor"),
        P("tensor", None),
        P("tensor", None),
        P(None, "tensor"),
    )
    out_specs = (P("dp", "tensor"), P("tensor", None), P(None, "tensor"))
    return jax.shard_map(
        per_device, mesh=mesh, in_specs=in_specs, out_specs=out_specs, check_vma=False
    )
```

```python
import jax
import jax.numpy as jnp
from jax import lax
from jax.experimental import pallas as pl
from jax.experimental.pallas import tpu as pltpu
from jax.sharding import PartitionSpec as P

SCALE = 2.0
RATE = 0.01
DAMPING = 0.01
RANK = 128
TOKENS = 1024
COLS = 256
HIDDEN = 924
SLOTS = 32
CHUNKS = 2
CHUNK = TOKENS // CHUNKS
DOWN_ROWS, UP_ROWS = 240, 64
STEP_ROWS = DOWN_ROWS + UP_ROWS
BLOCK = 64
GRAM_ROWS = 32
MESH = pl.DeviceIdType.MESH
HIGHEST = lax.Precision.HIGHEST

ORDER = (
    (0, 0), (-1, 0), (1, 0), (2, 0), (0, -1), (0, 1), (-1, -1), (-1, 1), (1, -1), (1, 1),
    (0, 2), (2, -1), (2, 1), (-1, 2), (1, 2), (2, 2),
)
LAST = 15
PRODUCTS = (
    (0, 0), (1, 0), (0, 1), (0, 2), (1, 1), (1, 2), (0, 3), (1, 3), (0, 4), (0, 5), (1, 4), (1, 5),
    (0, 6), (0, 7), (1, 6), (1, 7), (0, 8), (0, 9), (1, 8), (1, 9), (0, 10), (1, 10),
    (0, 11), (0, 12), (1, 11), (1, 12), (0, 13), (1, 13), (0, 14), (1, 14),
)
INVERT_FROM, INVERT_TO = 10, 26


def dot(left, right, dims_left, dims_right, precision=None):
    return lax.dot_general(
        left,
        right,
        (((dims_left,), (dims_right,)), ((), ())),
        precision=precision,
        preferred_element_type=jnp.float32,
    )


def eliminate(mat, count):
    lane = lax.broadcasted_iota(jnp.int32, (RANK, RANK), 1)
    row_of = lax.broadcasted_iota(jnp.int32, (RANK, RANK), 0)
    lane_row = lax.broadcasted_iota(jnp.int32, (1, RANK), 1)
    for j in range(count):
        column = jnp.broadcast_to(mat[:, j : j + 1], (RANK, RANK))
        inverse = 1.0 / column[j : j + 1, :]
        row = jnp.where(lane_row == j, inverse, mat[j : j + 1, :] * inverse)
        base = jnp.where((lane == j) | (row_of == j), 0.0, mat)
        mat = base - jnp.where(row_of == j, -1.0, column) * row
    mat = jnp.concatenate([mat[count:], mat[:count]], axis=0)
    return pltpu.roll(mat, RANK - count, axis=1)


def kernel(
    hidden_hbm, grad_hbm, weight_hbm, down_hbm, up_hbm,
    out_hbm, step_down_hbm, step_up_hbm,
    buf, weight, hidden, down, up, down16, acc, out16,
    part, from_sib, chip_sum, ring1, quarter, ring2, sum16, half16,
    gram_part, gram_sib, gram_sum, gram_in, gram,
    inverse, grads, grads_in, steps, step_down, step_up,
    local_sem, send_sem, slot_sem, misc_sem,
):
    dp = lax.axis_index("dp")
    me = lax.axis_index("tensor")
    core = lax.rem(me, 2)
    z = lax.rem(me // 2, 4)
    x = me // 8
    other = 1 - core
    a = x + core * (z - x)
    b = z + core * (x - z)

    def mod4(v):
        return lax.rem(v + 8, 4)

    def place(core_, a_, b_):
        return mod4(a_) * (8 - 6 * core_) + mod4(b_) * (2 + 6 * core_) + core_

    sib = me + 1 - 2 * core
    own = [place(core, a + da, b + db) for da, db in ORDER]
    theirs = [place(other, b + da, a + db) for da, db in ORDER]
    along_a = [(dp, place(core, a + d, b)) for d in (1, -1, 2)]
    along_b = [(dp, place(core, a, b + d)) for d in (1, -1, 2)]
    along_y = [(mod4(dp + d), me) for d in (1, -1, 2)]
    sibling = (dp, sib)
    a_plus, a_minus = along_a[0], along_a[1]
    b_plus, b_minus = along_b[0], along_b[1]

    def local(src, dst, sem):
        return pltpu.make_async_copy(src, dst, local_sem.at[sem])

    loads = [
        local(grad_hbm, buf.at[me], 0),
        local(up_hbm, up, 1),
        local(hidden_hbm, hidden, 2),
        local(down_hbm, down, 3),
        local(weight_hbm, weight, 4),
    ]
    for load in loads[:4]:
        load.start()

    barrier = pltpu.get_barrier_semaphore()
    cross_a = [(dp, place(other, b, a + d)) for d in (1, -1, 2)]
    cross_b = [(dp, place(other, b + d, a)) for d in (1, -1, 2)]
    partners = along_a + along_b + along_y + [sibling] + cross_a + cross_b
    for partner in partners:
        pl.semaphore_signal(barrier, inc=1, device_id=partner, device_id_type=MESH)

    pending = []

    def remote(refs, device):
        index = len(pending)

        def make(device):
            src, dst, recv_sem = refs()
            return pltpu.make_async_remote_copy(
                src_ref=src,
                dst_ref=dst,
                send_sem=send_sem.at[index],
                recv_sem=recv_sem,
                device_id=device,
                device_id_type=MESH,
            )

        pending.append(make)
        make(device).start()

    def landed(dst, recv_sem):
        pltpu.make_async_remote_copy(
            src_ref=dst,
            dst_ref=dst,
            send_sem=send_sem.at[0],
            recv_sem=recv_sem,
            device_id=sibling,
            device_id_type=MESH,
        ).wait_recv()

    def piece(slot, c):
        return buf.at[slot, pl.ds(c * CHUNK, CHUNK)]

    def pass_on(slot, c, device):
        remote(lambda: (piece(slot, c), piece(slot, c), slot_sem.at[slot, c]), device)

    def arrived(slot, c):
        landed(piece(slot, c), slot_sem.at[slot, c])

    SIB_PART, RING1, RING2, AG1, AG2, SIB_HALF, SIB_INV, Y_GRAD, Y_STEP = 0, 1, 5, 8, 12, 15, 16, 17, 20
    GRAM_SIB, GRAM_1, GRAM_Y = 23, 24, 32

    def own_first(c):
        pass_on(me, c, a_plus)
        pass_on(me, c, a_minus)

    loads[0].wait()
    loads[1].wait()
    up_f32 = up[...]
    part[0] = dot(buf[me], up_f32.astype(jnp.bfloat16), 1, 1).reshape(16, BLOCK, RANK)
    gram_part[0] = dot(up_f32, up_f32, 1, 1, HIGHEST).reshape(4, GRAM_ROWS, RANK)
    loads[2].wait()
    loads[3].wait()
    loads[4].start()
    down_f32 = down[...]
    down16[...] = down_f32.astype(jnp.bfloat16)
    gram_part[1] = dot(down_f32, down_f32, 0, 0, HIGHEST).reshape(4, GRAM_ROWS, RANK)
    part[1] = dot(down16[...], hidden[...], 0, 0).T.reshape(16, BLOCK, RANK)
    pl.semaphore_wait(barrier, len(partners))
    remote(lambda: (gram_part.at[other, dp], gram_sib, misc_sem.at[GRAM_SIB]), sibling)
    remote(lambda: (part.at[other], from_sib, misc_sem.at[SIB_PART]), sibling)
    own_first(0)
    own_first(1)
    for c in range(CHUNKS):
        pass_on(me, c, sibling)
    acc[...] = jnp.zeros_like(acc)

    def gram_stage(n, value):
        gram_sum[n] = value
        for j, device in enumerate(cross_b + [sibling]):
            remote(lambda j=j: (gram_sum.at[n], gram_in.at[n, j], misc_sem.at[GRAM_1 + 4 * n + j]), device)

    def gram_total(n):
        for j in range(4):
            landed(gram_in.at[n, j], misc_sem.at[GRAM_1 + 4 * n + j])
        return (gram_in[n, 0] + gram_in[n, 1]) + (gram_in[n, 2] + gram_in[n, 3])

    landed(gram_sib, misc_sem.at[GRAM_SIB])
    gram_stage(0, gram_part[core, dp] + gram_sib[...])
    landed(from_sib, misc_sem.at[SIB_PART])
    for j, (d, device) in enumerate(zip((1, -1, 2, 0), cross_a + [sibling])):
        rows = pl.ds(mod4(a + d) * 4, 4)
        chip_sum[rows] = part[core, rows] + from_sib[rows]
        remote(lambda j=j, rows=rows: (chip_sum.at[rows], ring1.at[j], misc_sem.at[RING1 + j]), device)

    def gram_first():
        gram_stage(1, gram_total(0))
        for c in range(CHUNKS):
            pass_on(me, c, b_plus)
            pass_on(me, c, b_minus)

    def gram_second():
        gram[dp] = gram_total(1)
        for j, device in enumerate(along_y):
            remote(lambda j=j: (gram.at[dp], gram.at[dp], misc_sem.at[GRAM_Y + j]), device)

    def gram_third():
        for j, d in enumerate((1, -1, 2)):
            landed(gram.at[mod4(dp - d)], misc_sem.at[GRAM_Y + j])
        eye = lax.broadcasted_iota(jnp.int32, (RANK, RANK), 0) == lax.broadcasted_iota(
            jnp.int32, (RANK, RANK), 1
        )
        inverse[core] = gram[...].reshape(RANK, RANK) + jnp.where(eye, DAMPING, 0.0)

    def reduce_first():
        for j in range(4):
            landed(ring1.at[j], misc_sem.at[RING1 + j])
        quarter[...] = (ring1[3] + ring1[0]) + (ring1[1] + ring1[2])
        for j, (d, device) in enumerate(zip((1, -1, 2), along_a)):
            remote(lambda j=j, d=d: (quarter.at[mod4(a + d)], ring2.at[j], misc_sem.at[RING2 + j]), device)

    def block(d):
        return a * 4 + mod4(b + d)

    def other_block():
        return b * 4 + a

    def rows_at(d):
        return pl.ds(mod4(a + d) * 4, 4)

    def reduce_second():
        for j in range(3):
            landed(ring2.at[j], misc_sem.at[RING2 + j])
        total = (quarter[a] + ring2[0]) + (ring2[1] + ring2[2])
        sum16[...] = total.astype(jnp.bfloat16)
        for j, device in enumerate(cross_a + [sibling]):
            remote(lambda j=j: (sum16, half16.at[other, other_block()], misc_sem.at[AG1 + j]), device)

    def gather_second():
        for j, d in enumerate((1, -1, 2, 0)):
            landed(half16.at[core, block(-d)], misc_sem.at[AG1 + j])
        for j, device in enumerate(along_a):
            remote(lambda j=j: (half16.at[core, rows_at(0)], half16.at[core, rows_at(0)], misc_sem.at[AG2 + j]), device)

    def share_sib():
        for j, d in enumerate((1, -1, 2)):
            landed(half16.at[core, rows_at(-d)], misc_sem.at[AG2 + j])
        remote(lambda: (half16.at[core], half16.at[core], misc_sem.at[SIB_HALF]), sibling)

    def form_grads():
        landed(half16.at[other], misc_sem.at[SIB_HALF])
        cotangent16 = half16[0].reshape(TOKENS, RANK)
        input16 = half16[1].reshape(TOKENS, RANK)
        grad_down = SCALE * dot(hidden[...], cotangent16, 1, 0)
        grad_up = SCALE * dot(input16, buf[me], 0, 0).T
        for q in range(4):
            last = min(DOWN_ROWS, HIDDEN - q * DOWN_ROWS)
            grads[q, 0:last] = grad_down[q * DOWN_ROWS : q * DOWN_ROWS + last]
            if last < DOWN_ROWS:
                grads[q, last:DOWN_ROWS] = jnp.zeros((DOWN_ROWS - last, RANK), jnp.float32)
            grads[q, DOWN_ROWS:STEP_ROWS] = grad_up[q * UP_ROWS : (q + 1) * UP_ROWS]
        for j, (d, device) in enumerate(zip((1, -1, 2), along_y)):
            remote(lambda j=j, d=d: (grads.at[mod4(dp + d)], grads_in.at[j], misc_sem.at[Y_GRAD + j]), device)
        acc[...] += dot(down16[...], cotangent16 * jnp.bfloat16(SCALE), 1, 1)

    def share_inverse():
        remote(lambda: (inverse.at[core], inverse.at[core], misc_sem.at[SIB_INV]), sibling)

    def solve():
        for j in range(3):
            landed(grads_in.at[j], misc_sem.at[Y_GRAD + j])
        total = RATE * ((grads[dp] + grads_in[0]) + (grads_in[1] + grads_in[2]))
        landed(inverse.at[other], misc_sem.at[SIB_INV])
        step_rows = dot(total[0:DOWN_ROWS], inverse[0], 1, 0, HIGHEST)
        steps[dp, 0:DOWN_ROWS] = step_rows.astype(jnp.bfloat16)
        step_rows = dot(total[DOWN_ROWS:STEP_ROWS], inverse[1], 1, 0, HIGHEST)
        steps[dp, DOWN_ROWS:STEP_ROWS] = step_rows.astype(jnp.bfloat16)
        for j, device in enumerate(along_y):
            remote(lambda j=j: (steps.at[dp], steps.at[dp], misc_sem.at[Y_STEP + j]), device)

    def receive_chunk(k, c):
        da, db = ORDER[k]
        arrived(own[k], c)
        if db == 0 and da == -1 and c == 0:
            pass_on(own[k], c, a_plus)
        if db == 0 and da == 1 and c == 1:
            pass_on(own[k], c, a_minus)
        if db == -1 and c == 0:
            pass_on(own[k], c, b_plus)
        if db == 1 and c == 1:
            pass_on(own[k], c, b_minus)
        if db == 0:
            pass_on(own[k], c, b_plus)
            pass_on(own[k], c, b_minus)
        pass_on(own[k], c, sibling)

    def receive(*blocks):
        for k in blocks:
            for c in range(CHUNKS):
                receive_chunk(k, c)

    stores = []

    def keep(make):
        stores.append(make)
        make().start()

    def finish_steps():
        for j, d in enumerate((1, -1, 2)):
            landed(steps.at[mod4(dp - d)], misc_sem.at[Y_STEP + j])
        step_down[...] = steps[:, 0:DOWN_ROWS, :].astype(jnp.float32).reshape(4 * DOWN_ROWS, RANK)
        keep(lambda: local(step_down.at[pl.ds(0, HIDDEN)], step_down_hbm, CHUNKS))
        step_up[...] = steps[:, DOWN_ROWS:STEP_ROWS, :].astype(jnp.float32).reshape(COLS, RANK).T
        keep(lambda: local(step_up, step_up_hbm, CHUNKS + 1))

    loads[4].wait()
    schedule = {
        1: [gram_first],
        2: [lambda: receive(1, 2)],
        4: [reduce_first],
        6: [lambda: receive(3)],
        7: [gram_second],
        8: [lambda: receive(4, 5), reduce_second],
        10: [gram_third],
        11: [gather_second],
        12: [lambda: receive(6, 7)],
        14: [share_sib],
        16: [lambda: receive(8, 9), form_grads],
        20: [lambda: receive(10)],
        22: [lambda: receive(11, 12)],
        26: [share_inverse, lambda: receive(13)],
        27: [solve],
        28: [lambda: receive(14)],
    }

    def pick(values, i):
        index = values[0]
        for k in range(1, len(values)):
            index = jnp.where(i == k, values[k], index)
        return index

    def columns(slot):
        return pl.ds(pl.multiple_of(slot * COLS, COLS), COLS)

    def step(i, carry):
        for k, events in schedule.items():

            @pl.when(i == k)
            def _(events=events):
                for event in events:
                    event()

        slot = pick([(own, theirs)[who][k] for who, k in PRODUCTS], i)
        from_other = pick([who for who, _ in PRODUCTS], i)

        @pl.when(from_other == 1)
        def _():
            for c in range(CHUNKS):
                arrived(slot, c)

        def multiply():
            acc[...] += dot(weight[:, columns(slot)], buf[slot], 1, 1)

        inverting = (i >= INVERT_FROM) & (i < INVERT_TO)

        @pl.when(inverting)
        def _():
            inverse[core] = eliminate(inverse[core], 8)
            multiply()

        @pl.when(jnp.logical_not(inverting))
        def _():
            multiply()

        return carry

    lax.fori_loop(0, len(PRODUCTS), step, 0)

    slot_own, slot_sib = own[LAST], theirs[LAST]
    for c in range(CHUNKS):
        arrived(slot_own, c)
        pass_on(slot_own, c, sibling)
    for c in range(CHUNKS):
        tokens = pl.ds(c * CHUNK, CHUNK)
        acc[:, tokens] += dot(weight[:, columns(slot_own)], buf[slot_own, tokens], 1, 1)
    for c in range(CHUNKS):
        tokens = pl.ds(c * CHUNK, CHUNK)
        arrived(slot_sib, c)
        last = dot(weight[:, columns(slot_sib)], buf[slot_sib, tokens], 1, 1)
        out16[:, tokens] = (acc[:, tokens] + last).astype(jnp.bfloat16)
        keep(lambda tokens=tokens, c=c: local(out16.at[:, tokens], out_hbm.at[:, tokens], c))
    finish_steps()
    for make in pending:
        make(sibling).wait_send()
    for make in stores:
        make().wait()


def copy_kernel(*refs):
    for source, target in zip(refs[:3], refs[3:]):
        target[...] = source[...]


def per_device(hidden_input, output_gradient, frozen_weight, adapter_down, adapter_up):
    f32, bf16 = jnp.float32, jnp.bfloat16
    any_space = pl.BlockSpec(memory_space=pl.ANY)
    results = pl.pallas_call(
        kernel,
        out_shape=(
            jax.ShapeDtypeStruct((HIDDEN, TOKENS), bf16),
            jax.ShapeDtypeStruct((HIDDEN, RANK), f32),
            jax.ShapeDtypeStruct((RANK, COLS), f32),
        ),
        in_specs=[any_space] * 5,
        out_specs=(any_space,) * 3,
        scratch_shapes=[
            pltpu.VMEM((SLOTS, TOKENS, COLS), bf16),
            pltpu.VMEM((HIDDEN, SLOTS * COLS), bf16),
            pltpu.VMEM((HIDDEN, TOKENS), bf16),
            pltpu.VMEM((HIDDEN, RANK), f32),
            pltpu.VMEM((RANK, COLS), f32),
            pltpu.VMEM((HIDDEN, RANK), bf16),
            pltpu.VMEM((HIDDEN, TOKENS), f32),
            pltpu.VMEM((HIDDEN, TOKENS), bf16),
            pltpu.VMEM((2, 16, BLOCK, RANK), f32),
            pltpu.VMEM((16, BLOCK, RANK), f32),
            pltpu.VMEM((16, BLOCK, RANK), f32),
            pltpu.VMEM((4, 4, BLOCK, RANK), f32),
            pltpu.VMEM((4, BLOCK, RANK), f32),
            pltpu.VMEM((3, BLOCK, RANK), f32),
            pltpu.VMEM((64, RANK), bf16),
            pltpu.VMEM((2, 16, 64, RANK), bf16),
            pltpu.VMEM((2, 4, GRAM_ROWS, RANK), f32),
            pltpu.VMEM((GRAM_ROWS, RANK), f32),
            pltpu.VMEM((2, GRAM_ROWS, RANK), f32),
            pltpu.VMEM((2, 4, GRAM_ROWS, RANK), f32),
            pltpu.VMEM((4, GRAM_ROWS, RANK), f32),
            pltpu.VMEM((2, RANK, RANK), f32),
            pltpu.VMEM((4, STEP_ROWS, RANK), f32),
            pltpu.VMEM((3, STEP_ROWS, RANK), f32),
            pltpu.VMEM((4, STEP_ROWS, RANK), bf16),
            pltpu.VMEM((4 * DOWN_ROWS, RANK), f32),
            pltpu.VMEM((RANK, COLS), f32),
            pltpu.SemaphoreType.DMA((CHUNKS + 5,)),
            pltpu.SemaphoreType.DMA((128,)),
            pltpu.SemaphoreType.DMA((SLOTS, CHUNKS)),
            pltpu.SemaphoreType.DMA((35,)),
        ],
        compiler_params=pltpu.CompilerParams(
            collective_id=0, has_side_effects=True, vmem_limit_bytes=60 * 2**20
        ),
    )(hidden_input.T, output_gradient, frozen_weight, adapter_down, adapter_up)
    specs = (
        pl.BlockSpec((HIDDEN, COLS), lambda i: (0, i)),
        pl.BlockSpec((DOWN_ROWS, RANK), lambda i: (i, 0)),
        pl.BlockSpec((RANK, COLS), lambda i: (0, 0)),
    )
    input_grad, step_down, step_up = pl.pallas_call(
        copy_kernel,
        grid=(4,),
        out_shape=tuple(jax.ShapeDtypeStruct(r.shape, r.dtype) for r in results),
        in_specs=specs,
        out_specs=specs,
    )(*results)
    return input_grad.T, step_down, step_up


def solution(mesh):
    in_specs = (
        P("dp", "tensor"),
        P("dp", "tensor"),
        P("tensor", None),
        P("tensor", None),
        P(None, "tensor"),
    )
    out_specs = (P("dp", "tensor"), P("tensor", None), P(None, "tensor"))
    return jax.shard_map(
        per_device, mesh=mesh, in_specs=in_specs, out_specs=out_specs, check_vma=False
    )
```

```python
import jax
import jax.numpy as jnp
from jax import lax
from jax.experimental import pallas as pl
from jax.experimental.pallas import tpu as pltpu
from jax.sharding import PartitionSpec as P

SCALE = 2.0
RATE = 0.01
DAMPING = 0.01
RANK = 128
TOKENS = 1024
COLS = 256
HIDDEN = 924
SLOTS = 32
CHUNKS = 2
CHUNK = TOKENS // CHUNKS
DOWN_ROWS, UP_ROWS = 240, 64
STEP_ROWS = DOWN_ROWS + UP_ROWS
BLOCK = 64
GRAM_ROWS = 32
MESH = pl.DeviceIdType.MESH
HIGHEST = lax.Precision.HIGHEST

ORDER = (
    (0, 0), (-1, 0), (1, 0), (0, -1), (0, 1), (2, 0), (-1, -1), (-1, 1), (1, -1), (1, 1),
    (0, 2), (2, -1), (2, 1), (-1, 2), (1, 2), (2, 2),
)
LAST = 15
PRODUCTS = (
    (0, 0), (1, 0), (0, 1), (0, 2), (1, 1), (1, 2), (0, 3), (0, 4), (1, 3), (1, 4), (0, 5), (1, 5),
    (0, 6), (0, 7), (1, 6), (1, 7), (0, 8), (0, 9), (1, 8), (1, 9), (0, 10), (1, 10),
    (0, 11), (0, 12), (1, 11), (1, 12), (0, 13), (1, 13), (0, 14), (1, 14),
)
INVERT_FROM, INVERT_TO = 10, 26


def dot(left, right, dims_left, dims_right, precision=None):
    return lax.dot_general(
        left,
        right,
        (((dims_left,), (dims_right,)), ((), ())),
        precision=precision,
        preferred_element_type=jnp.float32,
    )


def eliminate(mat, count):
    lane = lax.broadcasted_iota(jnp.int32, (RANK, RANK), 1)
    row_of = lax.broadcasted_iota(jnp.int32, (RANK, RANK), 0)
    lane_row = lax.broadcasted_iota(jnp.int32, (1, RANK), 1)
    for j in range(count):
        column = jnp.broadcast_to(mat[:, j : j + 1], (RANK, RANK))
        inverse = 1.0 / column[j : j + 1, :]
        row = jnp.where(lane_row == j, inverse, mat[j : j + 1, :] * inverse)
        base = jnp.where((lane == j) | (row_of == j), 0.0, mat)
        mat = base - jnp.where(row_of == j, -1.0, column) * row
    mat = jnp.concatenate([mat[count:], mat[:count]], axis=0)
    return pltpu.roll(mat, RANK - count, axis=1)


def kernel(
    hidden_hbm, grad_hbm, weight_hbm, down_hbm, up_hbm,
    out16, step_down, step_up,
    buf, weight, hidden, down, up, down16, acc,
    part, from_sib, chip_sum, ring1, quarter, ring2, sum16, half16,
    gram_part, gram_sib, gram_sum, gram_in, gram,
    inverse, grads, grads_in, steps,
    local_sem, send_sem, slot_sem, misc_sem,
):
    dp = lax.axis_index("dp")
    me = lax.axis_index("tensor")
    core = lax.rem(me, 2)
    z = lax.rem(me // 2, 4)
    x = me // 8
    other = 1 - core
    a = x + core * (z - x)
    b = z + core * (x - z)

    def mod4(v):
        return lax.rem(v + 8, 4)

    def place(core_, a_, b_):
        return mod4(a_) * (8 - 6 * core_) + mod4(b_) * (2 + 6 * core_) + core_

    sib = me + 1 - 2 * core
    own = [place(core, a + da, b + db) for da, db in ORDER]
    theirs = [place(other, b + da, a + db) for da, db in ORDER]
    along_a = [(dp, place(core, a + d, b)) for d in (1, -1, 2)]
    along_b = [(dp, place(core, a, b + d)) for d in (1, -1, 2)]
    along_y = [(mod4(dp + d), me) for d in (1, -1, 2)]
    sibling = (dp, sib)
    a_plus, a_minus = along_a[0], along_a[1]
    b_plus, b_minus = along_b[0], along_b[1]

    def local(src, dst, sem):
        return pltpu.make_async_copy(src, dst, local_sem.at[sem])

    loads = [
        local(grad_hbm, buf.at[me], 0),
        local(up_hbm, up, 1),
        local(hidden_hbm, hidden, 2),
        local(down_hbm, down, 3),
        local(weight_hbm, weight, 4),
    ]
    for load in loads[:4]:
        load.start()

    barrier = pltpu.get_barrier_semaphore()
    cross_a = [(dp, place(other, b, a + d)) for d in (1, -1, 2)]
    cross_b = [(dp, place(other, b + d, a)) for d in (1, -1, 2)]
    partners = along_a + along_b + along_y + [sibling] + cross_a + cross_b
    for partner in partners:
        pl.semaphore_signal(barrier, inc=1, device_id=partner, device_id_type=MESH)

    pending = []

    def remote(refs, device):
        index = len(pending)

        def make(device):
            src, dst, recv_sem = refs()
            return pltpu.make_async_remote_copy(
                src_ref=src,
                dst_ref=dst,
                send_sem=send_sem.at[index],
                recv_sem=recv_sem,
                device_id=device,
                device_id_type=MESH,
            )

        pending.append(make)
        make(device).start()

    def landed(dst, recv_sem):
        pltpu.make_async_remote_copy(
            src_ref=dst,
            dst_ref=dst,
            send_sem=send_sem.at[0],
            recv_sem=recv_sem,
            device_id=sibling,
            device_id_type=MESH,
        ).wait_recv()

    def piece(slot, c):
        return buf.at[slot, pl.ds(c * CHUNK, CHUNK)]

    def pass_on(slot, c, device):
        remote(lambda: (piece(slot, c), piece(slot, c), slot_sem.at[slot, c]), device)

    def arrived(slot, c):
        landed(piece(slot, c), slot_sem.at[slot, c])

    SIB_PART, RING1, RING2, AG1, AG2, SIB_HALF, SIB_INV, Y_GRAD, Y_STEP = 0, 1, 5, 8, 12, 15, 16, 17, 20
    GRAM_SIB, GRAM_1, GRAM_Y = 23, 24, 32

    def own_first(c):
        pass_on(me, c, a_plus)
        pass_on(me, c, a_minus)

    loads[0].wait()
    loads[1].wait()
    up_f32 = up[...]
    part[0] = dot(buf[me], up_f32.astype(jnp.bfloat16), 1, 1).reshape(16, BLOCK, RANK)
    gram_part[0] = dot(up_f32, up_f32, 1, 1, HIGHEST).reshape(4, GRAM_ROWS, RANK)
    loads[2].wait()
    loads[3].wait()
    loads[4].start()
    down_f32 = down[...]
    down16[...] = down_f32.astype(jnp.bfloat16)
    gram_part[1] = dot(down_f32, down_f32, 0, 0, HIGHEST).reshape(4, GRAM_ROWS, RANK)
    part[1] = dot(down16[...], hidden[...], 0, 0).T.reshape(16, BLOCK, RANK)
    pl.semaphore_wait(barrier, len(partners))
    remote(lambda: (gram_part.at[other, dp], gram_sib, misc_sem.at[GRAM_SIB]), sibling)
    remote(lambda: (part.at[other], from_sib, misc_sem.at[SIB_PART]), sibling)
    own_first(0)
    own_first(1)
    for c in range(CHUNKS):
        pass_on(me, c, sibling)
    acc[...] = jnp.zeros_like(acc)

    def gram_stage(n, value):
        gram_sum[n] = value
        for j, device in enumerate(cross_b + [sibling]):
            remote(lambda j=j: (gram_sum.at[n], gram_in.at[n, j], misc_sem.at[GRAM_1 + 4 * n + j]), device)

    def gram_total(n):
        for j in range(4):
            landed(gram_in.at[n, j], misc_sem.at[GRAM_1 + 4 * n + j])
        return (gram_in[n, 0] + gram_in[n, 1]) + (gram_in[n, 2] + gram_in[n, 3])

    landed(gram_sib, misc_sem.at[GRAM_SIB])
    gram_stage(0, gram_part[core, dp] + gram_sib[...])
    landed(from_sib, misc_sem.at[SIB_PART])
    for j, (d, device) in enumerate(zip((1, -1, 2, 0), cross_a + [sibling])):
        rows = pl.ds(mod4(a + d) * 4, 4)
        chip_sum[rows] = part[core, rows] + from_sib[rows]
        remote(lambda j=j, rows=rows: (chip_sum.at[rows], ring1.at[j], misc_sem.at[RING1 + j]), device)

    def gram_first():
        gram_stage(1, gram_total(0))

    def own_second():
        for c in range(CHUNKS):
            pass_on(me, c, b_plus)
            pass_on(me, c, b_minus)

    def gram_second():
        gram[dp] = gram_total(1)
        for j, device in enumerate(along_y):
            remote(lambda j=j: (gram.at[dp], gram.at[dp], misc_sem.at[GRAM_Y + j]), device)

    def gram_third():
        for j, d in enumerate((1, -1, 2)):
            landed(gram.at[mod4(dp - d)], misc_sem.at[GRAM_Y + j])
        eye = lax.broadcasted_iota(jnp.int32, (RANK, RANK), 0) == lax.broadcasted_iota(
            jnp.int32, (RANK, RANK), 1
        )
        inverse[core] = gram[...].reshape(RANK, RANK) + jnp.where(eye, DAMPING, 0.0)

    def reduce_first():
        for j in range(4):
            landed(ring1.at[j], misc_sem.at[RING1 + j])
        quarter[...] = (ring1[3] + ring1[0]) + (ring1[1] + ring1[2])
        for j, (d, device) in enumerate(zip((1, -1, 2), along_a)):
            remote(lambda j=j, d=d: (quarter.at[mod4(a + d)], ring2.at[j], misc_sem.at[RING2 + j]), device)

    def block(d):
        return a * 4 + mod4(b + d)

    def other_block():
        return b * 4 + a

    def rows_at(d):
        return pl.ds(mod4(a + d) * 4, 4)

    def reduce_second():
        for j in range(3):
            landed(ring2.at[j], misc_sem.at[RING2 + j])
        total = (quarter[a] + ring2[0]) + (ring2[1] + ring2[2])
        sum16[...] = total.astype(jnp.bfloat16)
        for j, device in enumerate(cross_a + [sibling]):
            remote(lambda j=j: (sum16, half16.at[other, other_block()], misc_sem.at[AG1 + j]), device)

    def gather_second():
        for j, d in enumerate((1, -1, 2, 0)):
            landed(half16.at[core, block(-d)], misc_sem.at[AG1 + j])
        for j, device in enumerate(along_a):
            remote(lambda j=j: (half16.at[core, rows_at(0)], half16.at[core, rows_at(0)], misc_sem.at[AG2 + j]), device)

    def share_sib():
        for j, d in enumerate((1, -1, 2)):
            landed(half16.at[core, rows_at(-d)], misc_sem.at[AG2 + j])
        remote(lambda: (half16.at[core], half16.at[core], misc_sem.at[SIB_HALF]), sibling)

    def form_grads():
        landed(half16.at[other], misc_sem.at[SIB_HALF])
        cotangent16 = half16[0].reshape(TOKENS, RANK)
        input16 = half16[1].reshape(TOKENS, RANK)
        grad_down = SCALE * dot(hidden[...], cotangent16, 1, 0)
        grad_up = SCALE * dot(input16, buf[me], 0, 0).T
        for q in range(4):
            last = min(DOWN_ROWS, HIDDEN - q * DOWN_ROWS)
            grads[q, 0:last] = grad_down[q * DOWN_ROWS : q * DOWN_ROWS + last]
            if last < DOWN_ROWS:
                grads[q, last:DOWN_ROWS] = jnp.zeros((DOWN_ROWS - last, RANK), jnp.float32)
            grads[q, DOWN_ROWS:STEP_ROWS] = grad_up[q * UP_ROWS : (q + 1) * UP_ROWS]
        for j, (d, device) in enumerate(zip((1, -1, 2), along_y)):
            remote(lambda j=j, d=d: (grads.at[mod4(dp + d)], grads_in.at[j], misc_sem.at[Y_GRAD + j]), device)
        acc[...] += dot(down16[...], cotangent16 * jnp.bfloat16(SCALE), 1, 1)

    def share_inverse():
        remote(lambda: (inverse.at[core], inverse.at[core], misc_sem.at[SIB_INV]), sibling)

    def solve():
        for j in range(3):
            landed(grads_in.at[j], misc_sem.at[Y_GRAD + j])
        total = RATE * ((grads[dp] + grads_in[0]) + (grads_in[1] + grads_in[2]))
        landed(inverse.at[other], misc_sem.at[SIB_INV])
        step_rows = dot(total[0:DOWN_ROWS], inverse[0], 1, 0, HIGHEST)
        steps[dp, 0:DOWN_ROWS] = step_rows.astype(jnp.bfloat16)
        step_rows = dot(total[DOWN_ROWS:STEP_ROWS], inverse[1], 1, 0, HIGHEST)
        steps[dp, DOWN_ROWS:STEP_ROWS] = step_rows.astype(jnp.bfloat16)
        for j, device in enumerate(along_y):
            remote(lambda j=j: (steps.at[dp], steps.at[dp], misc_sem.at[Y_STEP + j]), device)

    def receive_chunk(k, c):
        da, db = ORDER[k]
        arrived(own[k], c)
        if db == 0 and da == -1 and c == 0:
            pass_on(own[k], c, a_plus)
        if db == 0 and da == 1 and c == 1:
            pass_on(own[k], c, a_minus)
        if db == -1 and c == 0:
            pass_on(own[k], c, b_plus)
        if db == 1 and c == 1:
            pass_on(own[k], c, b_minus)
        if db == 0:
            pass_on(own[k], c, b_plus)
            pass_on(own[k], c, b_minus)
        pass_on(own[k], c, sibling)

    def receive(*blocks):
        for k in blocks:
            for c in range(CHUNKS):
                receive_chunk(k, c)

    def finish_steps():
        for j, d in enumerate((1, -1, 2)):
            landed(steps.at[mod4(dp - d)], misc_sem.at[Y_STEP + j])
        rows = steps[:, 0:DOWN_ROWS, :].astype(jnp.float32).reshape(4 * DOWN_ROWS, RANK)
        step_down[...] = rows[0:HIDDEN]
        step_up[...] = steps[:, DOWN_ROWS:STEP_ROWS, :].astype(jnp.float32).reshape(COLS, RANK).T

    loads[4].wait()
    schedule = {
        1: [own_second],
        2: [gram_first, lambda: receive(1, 2)],
        5: [reduce_first],
        6: [lambda: receive(3, 4)],
        7: [gram_second],
        9: [reduce_second],
        10: [lambda: receive(5), gram_third],
        12: [gather_second, lambda: receive(6, 7)],
        15: [share_sib],
        16: [lambda: receive(8, 9)],
        17: [form_grads],
        20: [lambda: receive(10)],
        22: [lambda: receive(11, 12)],
        26: [share_inverse, lambda: receive(13)],
        27: [solve],
        28: [lambda: receive(14)],
    }

    def pick(values, i):
        if len(values) == 1:
            return values[0]
        half = 1 << ((len(values) - 1).bit_length() - 1)
        return jnp.where(i < half, pick(values[:half], i), pick(values[half:], i - half))

    def run_events(i, keys):
        if len(keys) == 1:

            @pl.when(i == keys[0])
            def _():
                for event in schedule[keys[0]]:
                    event()

            return
        half = len(keys) // 2

        @pl.when(i < keys[half])
        def _():
            run_events(i, keys[:half])

        @pl.when(i >= keys[half])
        def _():
            run_events(i, keys[half:])

    def columns(slot):
        return pl.ds(pl.multiple_of(slot * COLS, COLS), COLS)

    def step(i, carry):
        run_events(i, sorted(schedule))
        code = pick([(own, theirs)[who][k] + SLOTS * who for who, k in PRODUCTS], i)
        from_other = code // SLOTS
        slot = code - SLOTS * from_other

        @pl.when(from_other == 1)
        def _():
            for c in range(CHUNKS):
                arrived(slot, c)

        def multiply():
            acc[...] += dot(weight[:, columns(slot)], buf[slot], 1, 1)

        inverting = (i >= INVERT_FROM) & (i < INVERT_TO)

        @pl.when(inverting)
        def _():
            inverse[core] = eliminate(inverse[core], 8)
            multiply()

        @pl.when(jnp.logical_not(inverting))
        def _():
            multiply()

        return carry

    lax.fori_loop(0, len(PRODUCTS), step, 0)

    slot_own, slot_sib = own[LAST], theirs[LAST]
    for c in range(CHUNKS):
        arrived(slot_own, c)
        pass_on(slot_own, c, sibling)
    for c in range(CHUNKS):
        tokens = pl.ds(c * CHUNK, CHUNK)
        acc[:, tokens] += dot(weight[:, columns(slot_own)], buf[slot_own, tokens], 1, 1)
    for c in range(CHUNKS):
        tokens = pl.ds(c * CHUNK, CHUNK)
        arrived(slot_sib, c)
        last = dot(weight[:, columns(slot_sib)], buf[slot_sib, tokens], 1, 1)
        out16[:, tokens] = (acc[:, tokens] + last).astype(jnp.bfloat16)
    finish_steps()
    for make in pending:
        make(sibling).wait_send()


def per_device(hidden_input, output_gradient, frozen_weight, adapter_down, adapter_up):
    f32, bf16 = jnp.float32, jnp.bfloat16
    any_space = pl.BlockSpec(memory_space=pl.ANY)
    input_grad, step_down, step_up = pl.pallas_call(
        kernel,
        out_shape=(
            pltpu.VMEM((HIDDEN, TOKENS), bf16),
            pltpu.VMEM((HIDDEN, RANK), f32),
            pltpu.VMEM((RANK, COLS), f32),
        ),
        in_specs=[any_space] * 5,
        out_specs=(pl.BlockSpec(memory_space=pltpu.VMEM),) * 3,
        scratch_shapes=[
            pltpu.VMEM((SLOTS, TOKENS, COLS), bf16),
            pltpu.VMEM((HIDDEN, SLOTS * COLS), bf16),
            pltpu.VMEM((HIDDEN, TOKENS), bf16),
            pltpu.VMEM((HIDDEN, RANK), f32),
            pltpu.VMEM((RANK, COLS), f32),
            pltpu.VMEM((HIDDEN, RANK), bf16),
            pltpu.VMEM((HIDDEN, TOKENS), f32),
            pltpu.VMEM((2, 16, BLOCK, RANK), f32),
            pltpu.VMEM((16, BLOCK, RANK), f32),
            pltpu.VMEM((16, BLOCK, RANK), f32),
            pltpu.VMEM((4, 4, BLOCK, RANK), f32),
            pltpu.VMEM((4, BLOCK, RANK), f32),
            pltpu.VMEM((3, BLOCK, RANK), f32),
            pltpu.VMEM((64, RANK), bf16),
            pltpu.VMEM((2, 16, 64, RANK), bf16),
            pltpu.VMEM((2, 4, GRAM_ROWS, RANK), f32),
            pltpu.VMEM((GRAM_ROWS, RANK), f32),
            pltpu.VMEM((2, GRAM_ROWS, RANK), f32),
            pltpu.VMEM((2, 4, GRAM_ROWS, RANK), f32),
            pltpu.VMEM((4, GRAM_ROWS, RANK), f32),
            pltpu.VMEM((2, RANK, RANK), f32),
            pltpu.VMEM((4, STEP_ROWS, RANK), f32),
            pltpu.VMEM((3, STEP_ROWS, RANK), f32),
            pltpu.VMEM((4, STEP_ROWS, RANK), bf16),
            pltpu.SemaphoreType.DMA((CHUNKS + 5,)),
            pltpu.SemaphoreType.DMA((128,)),
            pltpu.SemaphoreType.DMA((SLOTS, CHUNKS)),
            pltpu.SemaphoreType.DMA((35,)),
        ],
        compiler_params=pltpu.CompilerParams(
            collective_id=0, has_side_effects=True, vmem_limit_bytes=52 * 2**20
        ),
    )(hidden_input.T, output_gradient, frozen_weight, adapter_down, adapter_up)
    return input_grad.T, step_down, step_up


def solution(mesh):
    in_specs = (
        P("dp", "tensor"),
        P("dp", "tensor"),
        P("tensor", None),
        P("tensor", None),
        P(None, "tensor"),
    )
    out_specs = (P("dp", "tensor"), P("tensor", None), P(None, "tensor"))
    return jax.shard_map(
        per_device, mesh=mesh, in_specs=in_specs, out_specs=out_specs, check_vma=False
    )
```

```python
import jax
import jax.numpy as jnp
from jax import lax
from jax.experimental import pallas as pl
from jax.experimental.pallas import tpu as pltpu
from jax.sharding import PartitionSpec as P

SCALE = 2.0
RATE = 0.01
DAMPING = 0.01
RANK = 128
TOKENS = 1024
COLS = 256
HIDDEN = 924
SLOTS = 32
CHUNKS = 2
CHUNK = TOKENS // CHUNKS
DOWN_ROWS, UP_ROWS = 240, 64
STEP_ROWS = DOWN_ROWS + UP_ROWS
BLOCK = 64
GRAM_ROWS = 32
MESH = pl.DeviceIdType.MESH
HIGHEST = lax.Precision.HIGHEST

ORDER = (
    (0, 0), (-1, 0), (1, 0), (0, -1), (0, 1), (2, 0), (-1, -1), (-1, 1), (1, -1), (1, 1),
    (0, 2), (2, -1), (2, 1), (-1, 2), (1, 2), (2, 2),
)
LAST = 15
PRODUCTS = (
    (0, 0), (1, 0), (0, 1), (0, 2), (1, 1), (1, 2), (0, 3), (0, 4), (1, 3), (1, 4), (0, 5), (1, 5),
    (0, 6), (0, 7), (1, 6), (1, 7), (0, 8), (0, 9), (1, 8), (1, 9), (0, 10), (1, 10),
    (0, 11), (0, 12), (1, 11), (1, 12), (0, 13), (1, 13), (0, 14), (1, 14),
)
INVERT_FROM, INVERT_TO = 9, 25


def dot(left, right, dims_left, dims_right, precision=None):
    return lax.dot_general(
        left,
        right,
        (((dims_left,), (dims_right,)), ((), ())),
        precision=precision,
        preferred_element_type=jnp.float32,
    )


def eliminate(mat, count):
    lane = lax.broadcasted_iota(jnp.int32, (RANK, RANK), 1)
    row_of = lax.broadcasted_iota(jnp.int32, (RANK, RANK), 0)
    lane_row = lax.broadcasted_iota(jnp.int32, (1, RANK), 1)
    for j in range(count):
        column = jnp.broadcast_to(mat[:, j : j + 1], (RANK, RANK))
        inverse = 1.0 / column[j : j + 1, :]
        row = jnp.where(lane_row == j, inverse, mat[j : j + 1, :] * inverse)
        base = jnp.where((lane == j) | (row_of == j), 0.0, mat)
        mat = base - jnp.where(row_of == j, -1.0, column) * row
    mat = jnp.concatenate([mat[count:], mat[:count]], axis=0)
    return pltpu.roll(mat, RANK - count, axis=1)


def kernel(
    hidden_hbm, grad_hbm, weight_hbm, down_hbm, up_hbm,
    out16, step_down, step_up,
    buf, weight, hidden, down, up, down16, acc,
    part, from_sib, chip_sum, ring1, quarter, ring2, sum16, half16,
    gram_part, gram_sib, gram_sum, gram_in, gram,
    inverse, grads, grads_in, steps,
    local_sem, send_sem, slot_sem, misc_sem,
):
    dp = lax.axis_index("dp")
    me = lax.axis_index("tensor")
    core = lax.rem(me, 2)
    z = lax.rem(me // 2, 4)
    x = me // 8
    other = 1 - core
    a = x + core * (z - x)
    b = z + core * (x - z)

    def mod4(v):
        return lax.rem(v + 8, 4)

    def place(core_, a_, b_):
        return mod4(a_) * (8 - 6 * core_) + mod4(b_) * (2 + 6 * core_) + core_

    sib = me + 1 - 2 * core
    own = [place(core, a + da, b + db) for da, db in ORDER]
    theirs = [place(other, b + da, a + db) for da, db in ORDER]
    along_a = [(dp, place(core, a + d, b)) for d in (1, -1, 2)]
    along_b = [(dp, place(core, a, b + d)) for d in (1, -1, 2)]
    along_y = [(mod4(dp + d), me) for d in (1, -1, 2)]
    sibling = (dp, sib)
    a_plus, a_minus = along_a[0], along_a[1]
    b_plus, b_minus = along_b[0], along_b[1]

    def local(src, dst, sem):
        return pltpu.make_async_copy(src, dst, local_sem.at[sem])

    loads = [
        local(grad_hbm, buf.at[me], 0),
        local(up_hbm, up, 1),
        local(hidden_hbm, hidden, 2),
        local(down_hbm, down, 3),
        local(weight_hbm, weight, 4),
    ]
    barrier = pltpu.get_barrier_semaphore()
    cross_a = [(dp, place(other, b, a + d)) for d in (1, -1, 2)]
    cross_b = [(dp, place(other, b + d, a)) for d in (1, -1, 2)]
    partners = along_a + along_b + along_y + [sibling] + cross_a + cross_b
    for partner in partners:
        pl.semaphore_signal(barrier, inc=1, device_id=partner, device_id_type=MESH)

    for load in loads[:4]:
        load.start()

    pending = []
    drained = [0]
    marks = {}

    def mark(name):
        marks[name] = len(pending)


    def remote(refs, device):
        index = len(pending)

        def make(device):
            src, dst, recv_sem = refs()
            return pltpu.make_async_remote_copy(
                src_ref=src,
                dst_ref=dst,
                send_sem=send_sem.at[index],
                recv_sem=recv_sem,
                device_id=device,
                device_id_type=MESH,
            )

        pending.append(make)
        make(device).start()

    def drain(until):
        while drained[0] < until:
            pending[drained[0]](sibling).wait_send()
            drained[0] += 1

    def landed(dst, recv_sem):
        pltpu.make_async_remote_copy(
            src_ref=dst,
            dst_ref=dst,
            send_sem=send_sem.at[0],
            recv_sem=recv_sem,
            device_id=sibling,
            device_id_type=MESH,
        ).wait_recv()

    def piece(slot, c):
        return buf.at[slot, pl.ds(c * CHUNK, CHUNK)]

    def pass_on(slot, c, device):
        remote(lambda: (piece(slot, c), piece(slot, c), slot_sem.at[slot, c]), device)

    def hand_over(slot):
        remote(lambda: (buf.at[slot], buf.at[slot], slot_sem.at[slot, 0]), sibling)

    def arrived(slot, c):
        landed(piece(slot, c), slot_sem.at[slot, c])

    SIB_PART, RING1, RING2, AG1, AG2, SIB_HALF, SIB_INV, Y_GRAD, Y_STEP = 0, 1, 5, 8, 12, 15, 16, 17, 20
    GRAM_SIB, GRAM_1, GRAM_Y = 23, 24, 32

    def own_first(c):
        pass_on(me, c, a_plus)
        pass_on(me, c, a_minus)

    loads[0].wait()
    loads[1].wait()
    up_f32 = up[...]
    part[0] = dot(buf[me], up_f32.astype(jnp.bfloat16), 1, 1).reshape(16, BLOCK, RANK)
    gram_part[0] = dot(up_f32, up_f32, 1, 1, HIGHEST).reshape(4, GRAM_ROWS, RANK)
    pl.semaphore_wait(barrier, len(partners))
    own_first(0)
    own_first(1)
    loads[2].wait()
    loads[3].wait()
    loads[4].start()
    down_f32 = down[...]
    down16[...] = down_f32.astype(jnp.bfloat16)
    gram_part[1] = dot(down_f32, down_f32, 0, 0, HIGHEST).reshape(4, GRAM_ROWS, RANK)
    remote(lambda: (gram_part.at[other, dp], gram_sib, misc_sem.at[GRAM_SIB]), sibling)
    part[1] = dot(down16[...], hidden[...], 0, 0).T.reshape(16, BLOCK, RANK)
    remote(lambda: (part.at[other], from_sib, misc_sem.at[SIB_PART]), sibling)
    hand_over(me)
    acc[...] = jnp.zeros_like(acc)

    def gram_stage(n, value):
        gram_sum[n] = value
        for j, device in enumerate(cross_b + [sibling]):
            remote(lambda j=j: (gram_sum.at[n], gram_in.at[n, j], misc_sem.at[GRAM_1 + 4 * n + j]), device)

    def gram_total(n):
        for j in range(4):
            landed(gram_in.at[n, j], misc_sem.at[GRAM_1 + 4 * n + j])
        return (gram_in[n, 0] + gram_in[n, 1]) + (gram_in[n, 2] + gram_in[n, 3])

    landed(gram_sib, misc_sem.at[GRAM_SIB])
    gram_stage(0, gram_part[core, dp] + gram_sib[...])
    landed(from_sib, misc_sem.at[SIB_PART])
    for j, (d, device) in enumerate(zip((1, -1, 2, 0), cross_a + [sibling])):
        rows = pl.ds(mod4(a + d) * 4, 4)
        chip_sum[rows] = part[core, rows] + from_sib[rows]
        remote(lambda j=j, rows=rows: (chip_sum.at[rows], ring1.at[j], misc_sem.at[RING1 + j]), device)

    def gram_first():
        gram_stage(1, gram_total(0))

    mark("first")

    def own_second(c):
        pass_on(me, c, b_plus)
        pass_on(me, c, b_minus)

    def gram_second():
        gram[dp] = gram_total(1)
        for j, device in enumerate(along_y):
            remote(lambda j=j: (gram.at[dp], gram.at[dp], misc_sem.at[GRAM_Y + j]), device)

    def gram_third():
        for j, d in enumerate((1, -1, 2)):
            landed(gram.at[mod4(dp - d)], misc_sem.at[GRAM_Y + j])
        eye = lax.broadcasted_iota(jnp.int32, (RANK, RANK), 0) == lax.broadcasted_iota(
            jnp.int32, (RANK, RANK), 1
        )
        inverse[core] = gram[...].reshape(RANK, RANK) + jnp.where(eye, DAMPING, 0.0)

    def reduce_first():
        for j in range(4):
            landed(ring1.at[j], misc_sem.at[RING1 + j])
        quarter[...] = (ring1[3] + ring1[0]) + (ring1[1] + ring1[2])
        for j, (d, device) in enumerate(zip((1, -1, 2), along_a)):
            remote(lambda j=j, d=d: (quarter.at[mod4(a + d)], ring2.at[j], misc_sem.at[RING2 + j]), device)

    def block(d):
        return a * 4 + mod4(b + d)

    def other_block():
        return b * 4 + a

    def rows_at(d):
        return pl.ds(mod4(a + d) * 4, 4)

    def reduce_second():
        for j in range(3):
            landed(ring2.at[j], misc_sem.at[RING2 + j])
        total = (quarter[a] + ring2[0]) + (ring2[1] + ring2[2])
        sum16[...] = total.astype(jnp.bfloat16)
        for j, device in enumerate(cross_a + [sibling]):
            remote(lambda j=j: (sum16, half16.at[other, other_block()], misc_sem.at[AG1 + j]), device)

    def gather_second():
        for j, d in enumerate((1, -1, 2, 0)):
            landed(half16.at[core, block(-d)], misc_sem.at[AG1 + j])
        for j, device in enumerate(along_a):
            remote(lambda j=j: (half16.at[core, rows_at(0)], half16.at[core, rows_at(0)], misc_sem.at[AG2 + j]), device)

    def share_sib():
        for j, d in enumerate((1, -1, 2)):
            landed(half16.at[core, rows_at(-d)], misc_sem.at[AG2 + j])
        remote(lambda: (half16.at[core], half16.at[core], misc_sem.at[SIB_HALF]), sibling)

    def form_grads():
        landed(half16.at[other], misc_sem.at[SIB_HALF])
        cotangent16 = half16[0].reshape(TOKENS, RANK)
        input16 = half16[1].reshape(TOKENS, RANK)
        grad_down = SCALE * dot(hidden[...], cotangent16, 1, 0)
        grad_up = SCALE * dot(input16, buf[me], 0, 0).T
        for q in range(4):
            last = min(DOWN_ROWS, HIDDEN - q * DOWN_ROWS)
            grads[q, 0:last] = grad_down[q * DOWN_ROWS : q * DOWN_ROWS + last]
            if last < DOWN_ROWS:
                grads[q, last:DOWN_ROWS] = jnp.zeros((DOWN_ROWS - last, RANK), jnp.float32)
            grads[q, DOWN_ROWS:STEP_ROWS] = grad_up[q * UP_ROWS : (q + 1) * UP_ROWS]
        for j, (d, device) in enumerate(zip((1, -1, 2), along_y)):
            remote(lambda j=j, d=d: (grads.at[mod4(dp + d)], grads_in.at[j], misc_sem.at[Y_GRAD + j]), device)
        acc[...] += dot(down16[...], cotangent16 * jnp.bfloat16(SCALE), 1, 1)

    def share_inverse():
        remote(lambda: (inverse.at[core], inverse.at[core], misc_sem.at[SIB_INV]), sibling)

    def solve():
        for j in range(3):
            landed(grads_in.at[j], misc_sem.at[Y_GRAD + j])
        total = RATE * ((grads[dp] + grads_in[0]) + (grads_in[1] + grads_in[2]))
        landed(inverse.at[other], misc_sem.at[SIB_INV])
        step_rows = dot(total[0:DOWN_ROWS], inverse[0], 1, 0, HIGHEST)
        steps[dp, 0:DOWN_ROWS] = step_rows.astype(jnp.bfloat16)
        step_rows = dot(total[DOWN_ROWS:STEP_ROWS], inverse[1], 1, 0, HIGHEST)
        steps[dp, DOWN_ROWS:STEP_ROWS] = step_rows.astype(jnp.bfloat16)
        for j, device in enumerate(along_y):
            remote(lambda j=j: (steps.at[dp], steps.at[dp], misc_sem.at[Y_STEP + j]), device)

    def receive_chunk(k, c):
        da, db = ORDER[k]
        arrived(own[k], c)
        if db == 0 and da == -1 and c == 0:
            pass_on(own[k], c, a_plus)
        if db == 0 and da == 1 and c == 1:
            pass_on(own[k], c, a_minus)
        if db == -1 and c == 0:
            pass_on(own[k], c, b_plus)
        if db == 1 and c == 1:
            pass_on(own[k], c, b_minus)
        if db == 0:
            pass_on(own[k], c, b_plus)
            pass_on(own[k], c, b_minus)

    def receive(*blocks):
        for c in range(CHUNKS):
            for k in blocks:
                receive_chunk(k, c)
                if c == CHUNKS - 1:
                    hand_over(own[k])

    def finish_steps():
        for j, d in enumerate((1, -1, 2)):
            landed(steps.at[mod4(dp - d)], misc_sem.at[Y_STEP + j])
        rows = steps[:, 0:DOWN_ROWS, :].astype(jnp.float32).reshape(4 * DOWN_ROWS, RANK)
        step_down[...] = rows[0:HIDDEN]
        step_up[...] = steps[:, DOWN_ROWS:STEP_ROWS, :].astype(jnp.float32).reshape(COLS, RANK).T

    loads[4].wait()
    schedule = {
        0: [lambda: own_second(0)],
        1: [lambda: own_second(1)],
        2: [gram_first, lambda: receive(1, 2)],
        5: [reduce_first],
        6: [lambda: mark("second"), lambda: drain(marks["first"]), lambda: receive(3, 4)],
        7: [gram_second],
        9: [reduce_second, gram_third],
        10: [lambda: receive(5)],
        12: [gather_second, lambda: receive(6, 7)],
        15: [lambda: mark("third"), lambda: drain(marks["second"]), share_sib],
        16: [lambda: receive(8, 9)],
        17: [form_grads],
        20: [lambda: receive(10)],
        22: [lambda: receive(11, 12)],
        25: [share_inverse],
        26: [lambda: receive(13), lambda: drain(marks["third"]), solve],
        28: [lambda: receive(14)],
    }

    def pick(values, i):
        if len(values) == 1:
            return values[0]
        half = 1 << ((len(values) - 1).bit_length() - 1)
        return jnp.where(i < half, pick(values[:half], i), pick(values[half:], i - half))

    def run_events(i, keys):
        if len(keys) == 1:

            @pl.when(i == keys[0])
            def _():
                for event in schedule[keys[0]]:
                    event()

            return
        half = len(keys) // 2

        @pl.when(i < keys[half])
        def _():
            run_events(i, keys[:half])

        @pl.when(i >= keys[half])
        def _():
            run_events(i, keys[half:])

    def columns(slot):
        return pl.ds(pl.multiple_of(slot * COLS, COLS), COLS)

    def step(i, carry):
        run_events(i, sorted(schedule))
        code = pick([(own, theirs)[who][k] + SLOTS * who for who, k in PRODUCTS], i)
        from_other = code // SLOTS
        slot = code - SLOTS * from_other

        @pl.when(from_other == 1)
        def _():
            landed(buf.at[slot], slot_sem.at[slot, 0])

        def multiply():
            acc[...] += dot(weight[:, columns(slot)], buf[slot], 1, 1)

        inverting = (i >= INVERT_FROM) & (i < INVERT_TO)

        @pl.when(inverting)
        def _():
            inverse[core] = eliminate(inverse[core], 8)
            multiply()

        @pl.when(jnp.logical_not(inverting))
        def _():
            multiply()

        return carry

    lax.fori_loop(0, len(PRODUCTS), step, 0)

    slot_own, slot_sib = own[LAST], theirs[LAST]
    for c in range(CHUNKS):
        arrived(slot_own, c)
        pass_on(slot_own, c, sibling)
    for c in range(CHUNKS):
        tokens = pl.ds(c * CHUNK, CHUNK)
        acc[:, tokens] += dot(weight[:, columns(slot_own)], buf[slot_own, tokens], 1, 1)
    for c in range(CHUNKS):
        tokens = pl.ds(c * CHUNK, CHUNK)
        arrived(slot_sib, c)
        last = dot(weight[:, columns(slot_sib)], buf[slot_sib, tokens], 1, 1)
        out16[:, tokens] = (acc[:, tokens] + last).astype(jnp.bfloat16)
    finish_steps()
    drain(len(pending))


def per_device(hidden_input, output_gradient, frozen_weight, adapter_down, adapter_up):
    f32, bf16 = jnp.float32, jnp.bfloat16
    any_space = pl.BlockSpec(memory_space=pl.ANY)
    input_grad, step_down, step_up = pl.pallas_call(
        kernel,
        out_shape=(
            pltpu.VMEM((HIDDEN, TOKENS), bf16),
            pltpu.VMEM((HIDDEN, RANK), f32),
            pltpu.VMEM((RANK, COLS), f32),
        ),
        in_specs=[any_space] * 5,
        out_specs=(pl.BlockSpec(memory_space=pltpu.VMEM),) * 3,
        scratch_shapes=[
            pltpu.VMEM((SLOTS, TOKENS, COLS), bf16),
            pltpu.VMEM((HIDDEN, SLOTS * COLS), bf16),
            pltpu.VMEM((HIDDEN, TOKENS), bf16),
            pltpu.VMEM((HIDDEN, RANK), f32),
            pltpu.VMEM((RANK, COLS), f32),
            pltpu.VMEM((HIDDEN, RANK), bf16),
            pltpu.VMEM((HIDDEN, TOKENS), f32),
            pltpu.VMEM((2, 16, BLOCK, RANK), f32),
            pltpu.VMEM((16, BLOCK, RANK), f32),
            pltpu.VMEM((16, BLOCK, RANK), f32),
            pltpu.VMEM((4, 4, BLOCK, RANK), f32),
            pltpu.VMEM((4, BLOCK, RANK), f32),
            pltpu.VMEM((3, BLOCK, RANK), f32),
            pltpu.VMEM((64, RANK), bf16),
            pltpu.VMEM((2, 16, 64, RANK), bf16),
            pltpu.VMEM((2, 4, GRAM_ROWS, RANK), f32),
            pltpu.VMEM((GRAM_ROWS, RANK), f32),
            pltpu.VMEM((2, GRAM_ROWS, RANK), f32),
            pltpu.VMEM((2, 4, GRAM_ROWS, RANK), f32),
            pltpu.VMEM((4, GRAM_ROWS, RANK), f32),
            pltpu.VMEM((2, RANK, RANK), f32),
            pltpu.VMEM((4, STEP_ROWS, RANK), f32),
            pltpu.VMEM((3, STEP_ROWS, RANK), f32),
            pltpu.VMEM((4, STEP_ROWS, RANK), bf16),
            pltpu.SemaphoreType.DMA((CHUNKS + 5,)),
            pltpu.SemaphoreType.DMA((128,)),
            pltpu.SemaphoreType.DMA((SLOTS, CHUNKS)),
            pltpu.SemaphoreType.DMA((35,)),
        ],
        compiler_params=pltpu.CompilerParams(
            collective_id=0, has_side_effects=True, vmem_limit_bytes=52 * 2**20
        ),
    )(hidden_input.T, output_gradient, frozen_weight, adapter_down, adapter_up)
    return input_grad.T, step_down, step_up


def solution(mesh):
    in_specs = (
        P("dp", "tensor"),
        P("dp", "tensor"),
        P("tensor", None),
        P("tensor", None),
        P(None, "tensor"),
    )
    out_specs = (P("dp", "tensor"), P("tensor", None), P(None, "tensor"))
    return jax.shard_map(
        per_device, mesh=mesh, in_specs=in_specs, out_specs=out_specs, check_vma=False
    )
```
